128 devices in a mesh: attn: 16 (over z, x), exp: 8 (over y, core).
Axes of the slice: x: 4, y: 4, z: 4, core: 2. Of those that a mesh axis runs over, the one named last changes fastest.
Arguments:
- hidden_in: bfloat16 [128, 4096], P(('attn', 'exp')), may hold values from -6 to 6
- query: bfloat16 [128, 4096], P(('attn', 'exp')), may hold values from -240 to 240, as said below
- key_latent: bfloat16 [128, 1024, 512], P(('attn', 'exp')), may hold values from -6 to 6
- value_latent: bfloat16 [128, 1024, 512], P(('attn', 'exp')), may hold values from -6 to 6
- lengths: int32 [128], P(('attn', 'exp')), may hold values from 128 to 1024, as said below
- key_up: bfloat16 [512, 1024], replicated, may hold values from -0.25 to 0.25
- value_up: bfloat16 [512, 1024], replicated, may hold values from -0.25 to 0.25
- norm_gain: bfloat16 [4096], replicated, may hold values from 0.5 to 2
- router_weight: bfloat16 [4096, 8], replicated, may hold values from -0.09375 to 0.09375
- route_ids: int32 [128, 2], replicated, may hold values from 0 to 7, all different within a row; in each aligned block of 128 rows (0 to 127, 128 to 255, ...) at most 64 rows name the same one
- gate_weight: bfloat16 [8, 4096, 14336], P('exp', None, 'attn'), may hold values from -0.09375 to 0.09375
- up_weight: bfloat16 [8, 4096, 14336], P('exp', None, 'attn'), may hold values from -0.09375 to 0.09375
- down_weight: bfloat16 [8, 14336, 4096], P('exp', 'attn'), may hold values from -0.046875 to 0.046875
Outputs:
- mixed: bfloat16 [128, 4096], P(('attn', 'exp'))
The draws below stay inside these ranges and needn't reach their ends.
Inputs may be any that keep to these rules, and one draw needn't show every extreme that they name: `query`: query rows of order one; a row of a head may carry a common scale of up to some tens. `lengths`: in every draw one request has all 1024 slots live and one has 128. `route_ids`: A token's 2 experts differ; no expert is named by more than 64 tokens, a bound that some block reaches.
All inputs are finite; a program needn't handle non-finite values.
Results may differ from the reference program's by a relative error of at most 0.023.
Values may be sent and summed in bfloat16 or wider, within the bound.
No kernel may reach another device: no remote copies, remote signals or barrier semaphores. Data moves between devices by JAX's collectives and lax.ppermute only.
A program may use at most 128 MiB of HBM per device.

```python
import math
import jax
import jax.numpy as jnp
import numpy as np
from jax import lax

D = 4096
FF = 14336
HEADS = 32
KV_HEADS = 8
HEAD_DIM = 128
EXPERTS = 8
TOP = 2
RANK = 512
CTX = 1024
TOKENS = 128
CAP = 64


def draw_query(key, part):
    key = jax.random.fold_in(key, 11)
    base_values = jax.random.normal(key, (TOKENS, HEADS, HEAD_DIM), jnp.float32)
    base_values = jnp.clip(base_values, -6.0, 6.0)
    return base_values.reshape(TOKENS, HEADS * HEAD_DIM).astype(jnp.bfloat16)


def draw_lengths(key, part):
    key = jax.random.fold_in(key, 23)
    first_key, second_key, third_key = jax.random.split(key, 3)
    counts = jax.random.randint(first_key, (TOKENS,), CTX // 8, CTX + 1, jnp.int32)
    longest = jax.random.randint(second_key, (), 0, TOKENS, jnp.int32)
    shortest = (longest + 1 + jax.random.randint(third_key, (), 0, TOKENS - 1, jnp.int32)) % TOKENS
    counts = counts.at[longest].set(CTX)
    counts = counts.at[shortest].set(CTX // 8)
    return counts.astype(jnp.int32)


def steps_of(rng, extent, pieces, least, top_value):
    gain = 1.0
    for position, parts in pieces:
        draws = jax.random.uniform(jax.random.fold_in(jax.random.fold_in(rng, 6), position), (parts,), jnp.float32, least / len(pieces), top_value / len(pieces))
        gain = gain * jnp.repeat(jnp.exp(draws), extent[position] // parts).reshape((-1,) + (1,) * (len(extent) - 1 - position))
    return gain


def routed_block(own_key, own, number, rows, amount, top, most, lean):
    order = jax.random.permutation(own_key, amount)
    crowded, usual = portions_of(amount, rows * top, most, lean, True), portions_of(amount, rows * top, most, lean, False)
    places = jnp.arange(amount)

    def named(sizes, rotation):
        used = int((sizes > 0).sum())
        fixed = max(1, used // 4)
        shifted = fixed + (places - fixed + rotation * (used - fixed)) % max(1, amount - fixed)
        return jnp.zeros((amount,), jnp.int32).at[order[jnp.where(places < fixed, places, shifted)]].set(jnp.asarray(sizes, jnp.int32))

    sizes = jnp.where(number % 4 == 0, named(crowded, number // 4), named(usual, number - number // 4 - 1))
    mixed = jax.random.permutation(jax.random.fold_in(own, 3), amount)
    donor, taker = mixed[0:amount // 2 * 2:2], mixed[1:amount // 2 * 2:2]
    slack = jnp.minimum(sizes[donor] - 1, most - sizes[taker]) // 2
    slack = jnp.where((donor == order[0]) | (taker == order[0]) | (sizes[taker] == 0), 0, jnp.maximum(slack, 0))
    shifted = jax.random.randint(jax.random.fold_in(own, 4), (amount // 2,), 0, 1 << 20) % (slack + 1)
    sizes = sizes.at[donor].add(-shifted).at[taker].add(shifted)
    labels = jnp.searchsorted(jnp.cumsum(sizes), jnp.arange(rows * top), side="right").astype(jnp.int32)
    listing = labels.reshape(top, rows).T
    listing = listing[jax.random.permutation(jax.random.fold_in(own, 1), rows)]
    rotation = jax.random.randint(jax.random.fold_in(own, 2), (rows, 1), 0, top)
    return jnp.take_along_axis(listing, (jnp.arange(top)[None, :] + rotation) % top, axis=1)


def portions_of(number_of, total, most, slope, full):
    portions = [(1 << 20) // math.isqrt(grade ** slope) + 1 for grade in range(1, number_of + 1)]
    largest = most if full else min(most, max(-(-total // number_of), total * portions[0] // sum(portions)))
    least = 1 if total - largest >= number_of - 1 else 0
    given, rest = [largest] + [least] * (number_of - 1), total - largest - least * (number_of - 1)
    while rest > 0:
        candidates = [i for i in range(1, number_of) if given[i] < largest] or [i for i in range(1, number_of) if given[i] < most]
        mass, remaining = sum([portions[i] for i in candidates]), rest
        for i in candidates:
            extra = min(most - given[i], max(1, remaining * portions[i] // mass), rest)
            given[i] = given[i] + extra
            rest = rest - extra
    return np.array(given)


def centred(stream_key, extent, deviation, bound, pieces=(), held_as=jnp.bfloat16):
    result = deviation * jax.random.normal(stream_key, extent, jnp.float32)
    if pieces:
        result = result * steps_of(stream_key, extent, pieces, -0.22, 0.18)
    return jnp.clip(result, -bound, bound).astype(held_as)


def setup_inputs(seed: int = 0) -> dict:
    key_of = jax.random.split(jax.random.key(seed), 14)
    hidden_in = centred(key_of[0], (TOKENS, D), 1.0, 6.0, ((0, 128),))
    query = draw_query(jax.random.fold_in(key_of[13], 71), 0)
    key_latent = centred(key_of[2], (TOKENS, CTX, RANK), 1.0, 6.0, ((0, 128),))
    value_latent = centred(key_of[3], (TOKENS, CTX, RANK), 1.0, 6.0, ((0, 128),))
    lengths = draw_lengths(jax.random.fold_in(key_of[13], 71), 0)
    key_up = centred(key_of[5], (RANK, KV_HEADS * HEAD_DIM), RANK ** -0.5, 0.25)
    value_up = centred(key_of[6], (RANK, KV_HEADS * HEAD_DIM), RANK ** -0.5, 0.25)
    norm_gain = jnp.clip(jnp.exp(jax.random.uniform(key_of[7], (D,), jnp.float32, math.log(0.5), math.log(2.0))), 0.5, 2.0).astype(jnp.bfloat16)
    router_weight = centred(key_of[8], (D, EXPERTS), D ** -0.5, 0.09375)
    route_ids_keys = jax.random.split(jax.random.fold_in(key_of[9], 1), TOKENS // TOKENS)
    route_ids_turns = jax.random.permutation(jax.random.fold_in(key_of[9], 3), TOKENS // TOKENS)
    route_ids = jax.vmap(lambda own, number: routed_block(jax.random.fold_in(key_of[9], 2), own, number, TOKENS, EXPERTS, TOP, CAP, 2))(route_ids_keys, route_ids_turns).reshape((TOKENS, TOP))
    gate_weight = centred(key_of[10], (EXPERTS, D, FF), D ** -0.5, 0.09375, ((0, 8), (2, 16)))
    up_weight = centred(key_of[11], (EXPERTS, D, FF), D ** -0.5, 0.09375, ((0, 8), (2, 16)))
    down_weight = centred(key_of[12], (EXPERTS, FF, D), FF ** -0.5, 0.046875, ((0, 8), (1, 16)))
    return dict(hidden_in=hidden_in, query=query, key_latent=key_latent, value_latent=value_latent, lengths=lengths, key_up=key_up, value_up=value_up, norm_gain=norm_gain, router_weight=router_weight, route_ids=route_ids, gate_weight=gate_weight, up_weight=up_weight, down_weight=down_weight)


def attend_one(query_row, key_rows, value_rows, live_count, key_up, value_up):
    group = HEADS // KV_HEADS
    rebuilt_keys = jnp.dot(key_rows, key_up, preferred_element_type=jnp.float32).reshape(CTX, KV_HEADS, HEAD_DIM)
    rebuilt_values = jnp.dot(value_rows, value_up, preferred_element_type=jnp.float32).reshape(CTX, KV_HEADS, HEAD_DIM)
    query_heads = query_row.astype(jnp.float32).reshape(KV_HEADS, group, HEAD_DIM)
    scores = jnp.einsum('kgd,tkd->kgt', query_heads, rebuilt_keys, precision=lax.Precision.HIGHEST) * HEAD_DIM ** (-0.5)
    usable = jnp.arange(CTX) < live_count
    scores = jnp.where(usable[None, None, :], scores, jnp.float32(-1e+30))
    peak_score = lax.optimization_barrier(jnp.max(scores, axis=-1, keepdims=True))
    weights = jnp.where(usable[None, None, :], jnp.exp(scores - peak_score), jnp.float32(0.0))
    weights = weights / lax.optimization_barrier(jnp.sum(weights, axis=-1, keepdims=True))
    attended = jnp.einsum('kgt,tkd->kgd', weights, rebuilt_values, precision=lax.Precision.HIGHEST)
    return attended.reshape(D)

def reference(hidden_in, query, key_latent, value_latent, lengths, key_up, value_up, norm_gain, router_weight, route_ids, gate_weight, up_weight, down_weight):
    attended = lax.map(lambda packed: attend_one(packed[0], packed[1], packed[2], packed[3], key_up, value_up), (query, key_latent, value_latent, lengths))
    hidden = (hidden_in.astype(jnp.float32) + attended).astype(jnp.bfloat16)
    hidden_wide = hidden.astype(jnp.float32)
    scale_row = lax.rsqrt(lax.optimization_barrier(jnp.mean(hidden_wide * hidden_wide, axis=-1, keepdims=True)) + 1e-05)
    normed = (hidden_wide * scale_row * norm_gain.astype(jnp.float32)).astype(jnp.bfloat16)
    logits = jnp.dot(normed, router_weight, preferred_element_type=jnp.float32)
    chosen_logits = jnp.take_along_axis(logits, route_ids, axis=1)
    gates = jax.nn.softmax(chosen_logits, axis=1)

    def run_expert(expert_index):
        gate_part = jnp.dot(normed, gate_weight[expert_index], preferred_element_type=jnp.float32)
        up_part = jnp.dot(normed, up_weight[expert_index], preferred_element_type=jnp.float32)
        activation = (jax.nn.silu(gate_part) * up_part).astype(jnp.bfloat16)
        return jnp.dot(activation, down_weight[expert_index], preferred_element_type=jnp.float32).astype(jnp.bfloat16)
    expert_outputs = lax.map(run_expert, jnp.arange(EXPERTS))
    chosen_mask = (route_ids[:, :, None] == jnp.arange(EXPERTS)[None, None, :]).astype(jnp.float32)
    dense_gates = jnp.einsum('tk,tke->te', gates, chosen_mask, precision=lax.Precision.HIGHEST)
    combined = jnp.einsum('te,etd->td', dense_gates, expert_outputs.astype(jnp.float32), precision=lax.Precision.HIGHEST)
    return (hidden_wide + combined).astype(jnp.bfloat16)
```

```python
import jax
import jax.numpy as jnp
from jax import lax
from jax.experimental import pallas as pl
from jax.experimental.pallas import tpu as pltpu
from jax.sharding import Mesh, PartitionSpec as P

KV_HEADS = 8
GROUP = 4
HEAD_DIM = 128
RANK = 512
CTX = 1024
D = 4096
ROWS = 8
COLS = 512
CHIPS = 64
CHIP_AXES = ("z", "x", "y")
ALL_AXES = ("z", "x", "y", "core")
F32 = jnp.float32
BF16 = jnp.bfloat16
VMEM = pl.BlockSpec(memory_space=pltpu.VMEM)
SMEM = pl.BlockSpec(memory_space=pltpu.SMEM)


def parts_of(x, n):
    out = []
    for _ in range(n):
        p = x.astype(BF16)
        out.append(p)
        x = x - p.astype(F32)
    return out


def dot_nt(a, b):
    return lax.dot_general(a, b, (((1,), (1,)), ((), ())), preferred_element_type=F32)


def to_rows(ref, scratch):
    for s in range(ROWS):
        scratch[s : s + 1, :] = ref[0:1, s * COLS : (s + 1) * COLS].astype(F32)
    return scratch[...]


def attend_kernel(
    length, query, hidden_in, gain, key_latent, value_latent, key_up, value_up,
    sent, hidden_out, rows_scratch,
):
    q = to_rows(query, rows_scratch)
    kv_row = lax.broadcasted_iota(jnp.int32, (KV_HEADS, KV_HEADS * HEAD_DIM), 0)
    kv_col = lax.broadcasted_iota(jnp.int32, (KV_HEADS, KV_HEADS * HEAD_DIM), 1) // HEAD_DIM
    own_block = kv_row == kv_col
    spread = []
    for g in range(GROUP):
        piece = q[:, g * HEAD_DIM : (g + 1) * HEAD_DIM]
        spread.append(jnp.where(own_block, jnp.concatenate([piece] * KV_HEADS, axis=1), 0.0))
    spread = jnp.concatenate(spread, axis=0).astype(BF16)
    folded = dot_nt(spread, key_up[...])
    heads = KV_HEADS * GROUP
    stacked = jnp.concatenate(parts_of(folded, 3), axis=0)
    s3 = dot_nt(stacked, key_latent[0])
    scores = (s3[:heads] + s3[heads : 2 * heads] + s3[2 * heads :]) * HEAD_DIM ** (-0.5)
    usable = lax.broadcasted_iota(jnp.int32, (heads, CTX), 1) < length[0]
    scores = jnp.where(usable, scores, -1e30)
    peak = jnp.max(scores, axis=1, keepdims=True)
    weights = jnp.where(usable, jnp.exp(scores - peak), 0.0)
    total = jnp.sum(weights, axis=1, keepdims=True)
    w2 = jnp.concatenate(parts_of(weights, 2), axis=0)
    l2 = jnp.dot(w2, value_latent[0], preferred_element_type=F32)
    latent = (l2[:heads] + l2[heads:]) / total
    v2 = jnp.dot(jnp.concatenate(parts_of(latent, 2), axis=0), value_up[...], preferred_element_type=F32)
    values = v2[:heads] + v2[heads:]
    attended = []
    for g in range(GROUP):
        mine = jnp.where(own_block, values[g * KV_HEADS : (g + 1) * KV_HEADS], 0.0)
        acc = mine[:, :HEAD_DIM]
        for k in range(1, KV_HEADS):
            acc = acc + mine[:, k * HEAD_DIM : (k + 1) * HEAD_DIM]
        attended.append(acc)
    attended = jnp.concatenate(attended, axis=1)
    hidden = (to_rows(hidden_in, rows_scratch) + attended).astype(BF16).astype(F32)
    hidden_out[...] = hidden
    square = jnp.sum(jnp.sum(hidden * hidden, axis=1, keepdims=True), axis=0, keepdims=True)
    scale = lax.rsqrt(square * (1.0 / D) + 1e-05)
    normed = (hidden * scale * to_rows(gain, rows_scratch)).astype(BF16)
    sent[...] = jnp.broadcast_to(normed[None], sent.shape)


def expert_kernel(
    expert, own, other, ids, router, gate, up, down,
    out_own, out_other, wide, rows,
):
    half = CHIPS
    for i, block in enumerate((own, other)):
        wide[...] = block[...].astype(F32)
        for s in range(ROWS):
            rows[i * half : (i + 1) * half, s * COLS : (s + 1) * COLS] = wide[:, s, :].astype(BF16)
    x = rows[...]
    g = jnp.dot(x, gate[0], preferred_element_type=F32)
    u = jnp.dot(x, up[0], preferred_element_type=F32)
    act = (g * jax.nn.sigmoid(g) * u).astype(BF16)
    logits = jnp.dot(x, router[...], preferred_element_type=F32)
    lane = lax.broadcasted_iota(jnp.int32, logits.shape, 1)
    first, second = ids[:, 0:1], ids[:, 1:2]
    logit_a = jnp.sum(jnp.where(lane == first, logits, 0.0), axis=1, keepdims=True)
    logit_b = jnp.sum(jnp.where(lane == second, logits, 0.0), axis=1, keepdims=True)
    peak = jnp.maximum(logit_a, logit_b)
    exp_a, exp_b = jnp.exp(logit_a - peak), jnp.exp(logit_b - peak)
    mine = jnp.where(first == expert[0], exp_a, 0.0) + jnp.where(second == expert[0], exp_b, 0.0)
    weight = mine / (exp_a + exp_b)
    for i, out in enumerate((out_own, out_other)):
        for s in range(ROWS):
            part = jnp.dot(
                act[i * half : (i + 1) * half],
                down[0, :, s * COLS : (s + 1) * COLS],
                preferred_element_type=F32,
            )
            wide[:, s, :] = part * weight[i * half : (i + 1) * half]
        out[...] = wide[...].astype(BF16)


def add_kernel(a, b, out):
    out[...] = (a[...].astype(F32) + b[...].astype(F32)).astype(BF16)


def finish_kernel(parts, hidden, out):
    total = jnp.sum(parts[...].astype(F32), axis=0) + hidden[...]
    for s in range(ROWS):
        out[0:1, s * COLS : (s + 1) * COLS] = total[s : s + 1, :].astype(BF16)


def swap_cores(x):
    return lax.ppermute(x, "core", [(0, 1), (1, 0)])


def body(
    hidden_in, query, key_latent, value_latent, lengths, key_up, value_up,
    norm_gain, router_weight, route_ids, gate_weight, up_weight, down_weight,
):
    core = lax.axis_index("core")
    expert = lax.axis_index("y") * 2 + core
    token = jax.ShapeDtypeStruct((CHIPS, ROWS, COLS), BF16)
    sent, hidden = pl.pallas_call(
        attend_kernel,
        out_shape=(token, jax.ShapeDtypeStruct((ROWS, COLS), F32)),
        in_specs=[SMEM] + [VMEM] * 7,
        out_specs=(VMEM, VMEM),
        scratch_shapes=[pltpu.VMEM((ROWS, COLS), F32)],
        compiler_params=pltpu.CompilerParams(vmem_limit_bytes=24 * 2**20),
        name="attend",
    )(lengths, query, hidden_in, norm_gain.reshape(1, D), key_latent, value_latent, key_up, value_up)
    own = lax.all_to_all(sent, CHIP_AXES, 0, 0, tiled=True)
    other = swap_cores(own)
    by_chip = route_ids.reshape(CHIPS, 2, 2)
    ids = jnp.where(
        core == 0,
        jnp.concatenate([by_chip[:, 0], by_chip[:, 1]], axis=0),
        jnp.concatenate([by_chip[:, 1], by_chip[:, 0]], axis=0),
    )
    out_own, out_other = pl.pallas_call(
        expert_kernel,
        out_shape=(token, token),
        in_specs=[SMEM] + [VMEM] * 7,
        out_specs=(VMEM, VMEM),
        scratch_shapes=[
            pltpu.VMEM((CHIPS, ROWS, COLS), F32),
            pltpu.VMEM((2 * CHIPS, D), BF16),
        ],
        compiler_params=pltpu.CompilerParams(vmem_limit_bytes=48 * 2**20),
        name="experts",
    )(expert.reshape(1), own, other, ids, router_weight, gate_weight, up_weight, down_weight)
    summed = pl.pallas_call(
        add_kernel,
        out_shape=token,
        in_specs=[VMEM, VMEM],
        out_specs=VMEM,
        name="add_cores",
    )(out_own, swap_cores(out_other))
    parts = lax.all_to_all(summed, CHIP_AXES, 0, 0, tiled=True)
    return pl.pallas_call(
        finish_kernel,
        out_shape=jax.ShapeDtypeStruct((1, D), BF16),
        in_specs=[VMEM, VMEM],
        out_specs=VMEM,
        name="finish",
    )(parts, hidden)


def solution(mesh):
    fine = Mesh(mesh.devices.reshape(4, 4, 4, 2), ALL_AXES)
    in_specs = (
        P(ALL_AXES, None),
        P(ALL_AXES, None),
        P(ALL_AXES, None, None),
        P(ALL_AXES, None, None),
        P(ALL_AXES),
        P(),
        P(),
        P(),
        P(),
        P(),
        P(("y", "core"), None, ("z", "x")),
        P(("y", "core"), None, ("z", "x")),
        P(("y", "core"), ("z", "x"), None),
    )
    return jax.shard_map(
        body, mesh=fine, in_specs=in_specs, out_specs=P(ALL_AXES, None), check_vma=False
    )
```

```python
import jax
import jax.numpy as jnp
from jax import lax
from jax.experimental import pallas as pl
from jax.experimental.pallas import tpu as pltpu
from jax.sharding import Mesh, PartitionSpec as P

KV_HEADS = 8
GROUP = 4
HEADS = KV_HEADS * GROUP
HEAD_DIM = 128
RANK = 512
CTX = 1024
D = 4096
HIDDEN = 896
ROWS = 8
COLS = 512
CHIPS = 64
CHIP_AXES = ("z", "x", "y")
ALL_AXES = ("z", "x", "y", "core")
F32 = jnp.float32
BF16 = jnp.bfloat16
VMEM = pl.BlockSpec(memory_space=pltpu.VMEM)
SMEM = pl.BlockSpec(memory_space=pltpu.SMEM)
ANY = pl.BlockSpec(memory_space=pl.ANY)
MIB = 2**20
FIRST = 2048


def parts_of(x, n):
    out = []
    for _ in range(n):
        p = x.astype(BF16)
        out.append(p)
        x = x - p.astype(F32)
    return out


def dot_nt(a, b):
    return lax.dot_general(a, b, (((1,), (1,)), ((), ())), preferred_element_type=F32)


def dot(a, b):
    return jnp.dot(a, b, preferred_element_type=F32)


def to_rows(ref, scratch):
    for s in range(ROWS):
        scratch[s : s + 1, :] = ref[0:1, s * COLS : (s + 1) * COLS].astype(F32)
    return scratch[...]


def attend_kernel(
    length, query, hidden_in, gain, key_latent, value_latent, key_up, value_up,
    sent, hidden_out,
    rows_scratch, q_vmem, h_vmem, gain_vmem, kl_vmem, vl_vmem, ku_vmem, vu_vmem, small_sem, sem,
):
    small = [
        pltpu.make_async_copy(query, q_vmem, small_sem.at[0]),
        pltpu.make_async_copy(hidden_in, h_vmem, small_sem.at[1]),
        pltpu.make_async_copy(gain, gain_vmem, small_sem.at[2]),
    ]
    for c in small:
        c.start()
    big = [
        pltpu.make_async_copy(src, dst, sem.at[i])
        for i, (src, dst) in enumerate(
            ((key_up, ku_vmem), (key_latent.at[0], kl_vmem), (value_latent.at[0], vl_vmem), (value_up, vu_vmem))
        )
    ]
    big[0].start()
    big[1].start()
    for c in small:
        c.wait()
    big[2].start()
    big[3].start()

    q = to_rows(q_vmem, rows_scratch)
    kv_row = lax.broadcasted_iota(jnp.int32, (KV_HEADS, KV_HEADS * HEAD_DIM), 0)
    kv_col = lax.broadcasted_iota(jnp.int32, (KV_HEADS, KV_HEADS * HEAD_DIM), 1) // HEAD_DIM
    own_block = kv_row == kv_col
    spread = []
    for g in range(GROUP):
        piece = q[:, g * HEAD_DIM : (g + 1) * HEAD_DIM]
        spread.append(jnp.where(own_block, jnp.concatenate([piece] * KV_HEADS, axis=1), 0.0))
    spread = jnp.concatenate(spread, axis=0).astype(BF16)
    big[0].wait()
    folded = dot_nt(spread, ku_vmem[...])
    stacked = jnp.concatenate(parts_of(folded, 3), axis=0)
    big[1].wait()
    s3 = dot_nt(stacked, kl_vmem[...])
    scores = (s3[:HEADS] + s3[HEADS : 2 * HEADS] + s3[2 * HEADS :]) * HEAD_DIM ** (-0.5)
    usable = lax.broadcasted_iota(jnp.int32, (HEADS, CTX), 1) < length[0]
    scores = jnp.where(usable, scores, -1e30)
    peak = jnp.max(scores, axis=1, keepdims=True)
    weights = jnp.where(usable, jnp.exp(scores - peak), 0.0)
    total = jnp.sum(weights, axis=1, keepdims=True)
    w2 = jnp.concatenate(parts_of(weights, 2), axis=0)
    big[2].wait()
    l2 = dot(w2, vl_vmem[...])
    latent = (l2[:HEADS] + l2[HEADS:]) / total
    big[3].wait()
    v2 = dot(jnp.concatenate(parts_of(latent, 2), axis=0), vu_vmem[...])
    values = v2[:HEADS] + v2[HEADS:]
    attended = []
    for g in range(GROUP):
        mine = jnp.where(own_block, values[g * KV_HEADS : (g + 1) * KV_HEADS], 0.0)
        acc = mine[:, :HEAD_DIM]
        for k in range(1, KV_HEADS):
            acc = acc + mine[:, k * HEAD_DIM : (k + 1) * HEAD_DIM]
        attended.append(acc)
    attended = jnp.concatenate(attended, axis=1)
    hidden = (to_rows(h_vmem, rows_scratch) + attended).astype(BF16).astype(F32)
    hidden_out[...] = hidden
    square = jnp.sum(jnp.sum(hidden * hidden, axis=1, keepdims=True), axis=0, keepdims=True)
    scale = lax.rsqrt(square * (1.0 / D) + 1e-05)
    normed = (hidden * scale * gain_vmem[...].astype(F32).reshape(ROWS, COLS)).astype(BF16)
    sent[...] = jnp.broadcast_to(normed[None], sent.shape)


def gates_of(x, router, ids, parity, expert):
    shape = (2 * CHIPS, 2 * CHIPS)
    row = lax.broadcasted_iota(jnp.int32, shape, 0)
    other = (row >= CHIPS).astype(jnp.int32)
    token = 2 * (row - other * CHIPS) + (parity + other - 2 * parity * other)
    pick = (token == lax.broadcasted_iota(jnp.int32, shape, 1)).astype(F32).astype(BF16)
    wide_ids = jnp.concatenate([ids[...].astype(F32), jnp.zeros((6, 2 * CHIPS), F32)], axis=0).astype(BF16)
    mine = dot_nt(pick, wide_ids).astype(jnp.int32)
    first, second = mine[:, 0:1], mine[:, 1:2]
    logits = dot_nt(x, router[...])
    lane = lax.broadcasted_iota(jnp.int32, logits.shape, 1)
    logit_a = jnp.sum(jnp.where(lane == first, logits, 0.0), axis=1, keepdims=True)
    logit_b = jnp.sum(jnp.where(lane == second, logits, 0.0), axis=1, keepdims=True)
    peak = jnp.maximum(logit_a, logit_b)
    exp_a, exp_b = jnp.exp(logit_a - peak), jnp.exp(logit_b - peak)
    chosen = jnp.where(first == expert, exp_a, 0.0) + jnp.where(second == expert, exp_b, 0.0)
    return chosen / (exp_a + exp_b)


def load_kernel(after, gate, out, sem):
    copy = pltpu.make_async_copy(gate.at[0, pl.ds(0, FIRST)], out, sem)
    copy.start()
    copy.wait()


def expert_kernel(
    own, other, ids, router, gate_first, gate, up, down,
    out_own, out_other,
    rows, gate_rest, up_vmem, down_vmem, g_part, u_part, act, weight, sem,
):
    core = lax.axis_index("core")
    expert = 2 * lax.axis_index("y") + core
    step = pl.when(core >= 0)
    half = D // 2
    quarter = D // 4
    gate_copy = pltpu.make_async_copy(gate.at[0, pl.ds(FIRST, D - FIRST)], gate_rest, sem.at[0])
    up_copies = [
        pltpu.make_async_copy(
            up.at[0, pl.ds(j * half, half)], up_vmem.at[pl.ds(j * half, half)], sem.at[1 + j]
        )
        for j in range(2)
    ]
    down_copies = [
        pltpu.make_async_copy(
            down.at[0, :, pl.ds(j * quarter, quarter)], down_vmem.at[:, pl.ds(j * quarter, quarter)], sem.at[3 + j]
        )
        for j in range(4)
    ]
    for c in [gate_copy] + up_copies + down_copies:
        c.start()

    @step
    def _():
        rows[:CHIPS] = own[...].reshape(CHIPS, D)
        rows[CHIPS:] = other[...].reshape(CHIPS, D)

    @step
    def _():
        g_part[...] = dot(rows[:, :FIRST], gate_first[...])

    @step
    def _():
        weight[...] = jnp.broadcast_to(gates_of(rows[...], router, ids, core, expert), weight.shape)

    gate_copy.wait()

    @step
    def _():
        g_part[...] += dot(rows[:, FIRST:], gate_rest[...])

    up_copies[0].wait()

    @step
    def _():
        u_part[...] = dot(rows[:, :half], up_vmem[:half])

    up_copies[1].wait()

    @step
    def _():
        g = g_part[...]
        u = u_part[...] + dot(rows[:, half:], up_vmem[half:])
        act[...] = (g * jax.nn.sigmoid(g) * u).astype(BF16)

    for j, c in enumerate(down_copies):
        c.wait()

        @step
        def _(j=j):
            for s in (2 * j, 2 * j + 1):
                cols = slice(s * COLS, (s + 1) * COLS)
                rows[:, cols] = (dot(act[...], down_vmem[:, cols]) * weight[:, :1]).astype(BF16)

    @step
    def _():
        out_own[...] = rows[:CHIPS].reshape(out_own.shape)
        out_other[...] = rows[CHIPS:].reshape(out_other.shape)


def add_kernel(a, b, out):
    out[...] = (a[...].astype(F32) + b[...].astype(F32)).astype(BF16)


def finish_kernel(parts, hidden, out):
    total = jnp.sum(parts[...].astype(F32), axis=0) + hidden[...]
    for s in range(ROWS):
        out[0:1, s * COLS : (s + 1) * COLS] = total[s : s + 1, :].astype(BF16)


def swap_cores(x):
    return lax.ppermute(x, "core", [(0, 1), (1, 0)])


def params(mib):
    return pltpu.CompilerParams(vmem_limit_bytes=mib * MIB)


def in_vmem(x):
    return pltpu.with_memory_space_constraint(x, pltpu.VMEM)


def in_hbm(x):
    return pltpu.with_memory_space_constraint(x, pltpu.HBM)


def body(
    hidden_in, query, key_latent, value_latent, lengths, key_up, value_up,
    norm_gain, router_weight, route_ids, gate_weight, up_weight, down_weight,
):
    router = router_weight.T
    ids = route_ids.T
    block = (CHIPS, ROWS, COLS)
    token = jax.ShapeDtypeStruct(block, BF16)
    sent, hidden = pl.pallas_call(
        attend_kernel,
        out_shape=(token, jax.ShapeDtypeStruct((ROWS, COLS), F32)),
        in_specs=[SMEM] + [ANY] * 7,
        out_specs=(VMEM, VMEM),
        scratch_shapes=[
            pltpu.VMEM((ROWS, COLS), F32),
            pltpu.VMEM((1, D), BF16),
            pltpu.VMEM((1, D), BF16),
            pltpu.VMEM((D,), BF16),
            pltpu.VMEM((CTX, RANK), BF16),
            pltpu.VMEM((CTX, RANK), BF16),
            pltpu.VMEM((RANK, KV_HEADS * HEAD_DIM), BF16),
            pltpu.VMEM((RANK, KV_HEADS * HEAD_DIM), BF16),
            pltpu.SemaphoreType.DMA((3,)),
            pltpu.SemaphoreType.DMA((4,)),
        ],
        compiler_params=params(16),
        name="attend",
    )(
        lengths, in_hbm(query), in_hbm(hidden_in), in_hbm(norm_gain),
        in_hbm(key_latent), in_hbm(value_latent), in_hbm(key_up), in_hbm(value_up),
    )
    own = lax.all_to_all(sent, CHIP_AXES, 0, 0, tiled=True)
    other = swap_cores(own)
    gate_first = pl.pallas_call(
        load_kernel,
        out_shape=pltpu.VMEM((FIRST, HIDDEN), BF16),
        in_specs=[VMEM, ANY],
        out_specs=ANY,
        scratch_shapes=[pltpu.SemaphoreType.DMA],
        compiler_params=params(2),
        cost_estimate=pl.CostEstimate(flops=0, bytes_accessed=8 * MIB, transcendentals=0),
        name="load_gate",
    )(hidden, in_hbm(gate_weight))
    out_own, out_other = pl.pallas_call(
        expert_kernel,
        out_shape=(token, token),
        in_specs=[VMEM] * 5 + [ANY] * 3,
        out_specs=(VMEM, VMEM),
        scratch_shapes=[
            pltpu.VMEM((2 * CHIPS, D), BF16),
            pltpu.VMEM((D - FIRST, HIDDEN), BF16),
            pltpu.VMEM((D, HIDDEN), BF16),
            pltpu.VMEM((HIDDEN, D), BF16),
            pltpu.VMEM((2 * CHIPS, HIDDEN), F32),
            pltpu.VMEM((2 * CHIPS, HIDDEN), F32),
            pltpu.VMEM((2 * CHIPS, HIDDEN), BF16),
            pltpu.VMEM((2 * CHIPS, HEAD_DIM), F32),
            pltpu.SemaphoreType.DMA((7,)),
        ],
        compiler_params=params(32),
        name="experts",
    )(
        own, other, ids, router, in_vmem(gate_first),
        in_hbm(gate_weight), in_hbm(up_weight), in_hbm(down_weight),
    )
    from_other = swap_cores(out_other)
    summed = pl.pallas_call(
        add_kernel,
        out_shape=token,
        in_specs=[VMEM, VMEM],
        out_specs=VMEM,
        compiler_params=params(4),
        name="add_cores",
    )(out_own, from_other)
    parts = lax.all_to_all(summed, CHIP_AXES, 0, 0, tiled=True)
    return pl.pallas_call(
        finish_kernel,
        out_shape=jax.ShapeDtypeStruct((1, D), BF16),
        in_specs=[VMEM, VMEM],
        out_specs=VMEM,
        compiler_params=params(4),
        name="finish",
    )(parts, hidden)


def solution(mesh):
    fine = Mesh(mesh.devices.reshape(4, 4, 4, 2), ALL_AXES)
    in_specs = (
        P(ALL_AXES, None),
        P(ALL_AXES, None),
        P(ALL_AXES, None, None),
        P(ALL_AXES, None, None),
        P(ALL_AXES),
        P(),
        P(),
        P(),
        P(),
        P(),
        P(("y", "core"), None, ("z", "x")),
        P(("y", "core"), None, ("z", "x")),
        P(("y", "core"), ("z", "x"), None),
    )
    return jax.shard_map(
        body, mesh=fine, in_specs=in_specs, out_specs=P(ALL_AXES, None), check_vma=False
    )
```

```python
import jax
import jax.numpy as jnp
from jax import lax
from jax.experimental import pallas as pl
from jax.experimental.pallas import tpu as pltpu
from jax.sharding import Mesh, PartitionSpec as P

KV_HEADS = 8
GROUP = 4
HEADS = KV_HEADS * GROUP
HEAD_DIM = 128
RANK = 512
CTX = 1024
D = 4096
HIDDEN = 896
ROWS = 8
COLS = 512
CHIPS = 64
CHIP_AXES = ("z", "x", "y")
ALL_AXES = ("z", "x", "y", "core")
F32 = jnp.float32
BF16 = jnp.bfloat16
VMEM = pl.BlockSpec(memory_space=pltpu.VMEM)
SMEM = pl.BlockSpec(memory_space=pltpu.SMEM)
ANY = pl.BlockSpec(memory_space=pl.ANY)
MIB = 2**20


def parts_of(x, n):
    out = []
    for _ in range(n):
        p = x.astype(BF16)
        out.append(p)
        x = x - p.astype(F32)
    return out


def dot_nt(a, b):
    return lax.dot_general(a, b, (((1,), (1,)), ((), ())), preferred_element_type=F32)


def dot(a, b):
    return jnp.dot(a, b, preferred_element_type=F32)


def to_rows(ref, scratch):
    for s in range(ROWS):
        scratch[s : s + 1, :] = ref[0:1, s * COLS : (s + 1) * COLS].astype(F32)
    return scratch[...]


def attend_kernel(
    length, query, hidden_in, gain, key_latent, value_latent, key_up, value_up,
    normed_out, hidden_out,
    rows_scratch, q_vmem, h_vmem, gain_vmem, kl_vmem, vl_vmem, ku_vmem, vu_vmem, small_sem, sem,
):
    small = [
        pltpu.make_async_copy(query, q_vmem, small_sem.at[0]),
        pltpu.make_async_copy(hidden_in, h_vmem, small_sem.at[1]),
        pltpu.make_async_copy(gain, gain_vmem, small_sem.at[2]),
    ]
    for c in small:
        c.start()
    big = [
        pltpu.make_async_copy(src, dst, sem.at[i])
        for i, (src, dst) in enumerate(
            ((key_up, ku_vmem), (key_latent.at[0], kl_vmem), (value_latent.at[0], vl_vmem), (value_up, vu_vmem))
        )
    ]
    big[0].start()
    big[1].start()
    for c in small:
        c.wait()
    big[2].start()
    big[3].start()

    q = to_rows(q_vmem, rows_scratch)
    kv_row = lax.broadcasted_iota(jnp.int32, (KV_HEADS, KV_HEADS * HEAD_DIM), 0)
    kv_col = lax.broadcasted_iota(jnp.int32, (KV_HEADS, KV_HEADS * HEAD_DIM), 1) // HEAD_DIM
    own_block = kv_row == kv_col
    spread = []
    for g in range(GROUP):
        piece = q[:, g * HEAD_DIM : (g + 1) * HEAD_DIM]
        spread.append(jnp.where(own_block, jnp.concatenate([piece] * KV_HEADS, axis=1), 0.0))
    spread = jnp.concatenate(spread, axis=0).astype(BF16)
    big[0].wait()
    folded = dot_nt(spread, ku_vmem[...])
    stacked = jnp.concatenate(parts_of(folded, 3), axis=0)
    big[1].wait()
    s3 = dot_nt(stacked, kl_vmem[...])
    scores = (s3[:HEADS] + s3[HEADS : 2 * HEADS] + s3[2 * HEADS :]) * HEAD_DIM ** (-0.5)
    usable = lax.broadcasted_iota(jnp.int32, (HEADS, CTX), 1) < length[0]
    scores = jnp.where(usable, scores, -1e30)
    peak = jnp.max(scores, axis=1, keepdims=True)
    weights = jnp.where(usable, jnp.exp(scores - peak), 0.0)
    total = jnp.sum(weights, axis=1, keepdims=True)
    w2 = jnp.concatenate(parts_of(weights, 2), axis=0)
    big[2].wait()
    l2 = dot(w2, vl_vmem[...])
    latent = (l2[:HEADS] + l2[HEADS:]) / total
    big[3].wait()
    v2 = dot(jnp.concatenate(parts_of(latent, 2), axis=0), vu_vmem[...])
    values = v2[:HEADS] + v2[HEADS:]
    attended = []
    for g in range(GROUP):
        mine = jnp.where(own_block, values[g * KV_HEADS : (g + 1) * KV_HEADS], 0.0)
        acc = mine[:, :HEAD_DIM]
        for k in range(1, KV_HEADS):
            acc = acc + mine[:, k * HEAD_DIM : (k + 1) * HEAD_DIM]
        attended.append(acc)
    attended = jnp.concatenate(attended, axis=1)
    hidden = (to_rows(h_vmem, rows_scratch) + attended).astype(BF16).astype(F32)
    hidden_out[...] = hidden
    square = jnp.sum(jnp.sum(hidden * hidden, axis=1, keepdims=True), axis=0, keepdims=True)
    scale = lax.rsqrt(square * (1.0 / D) + 1e-05)
    normed = (hidden * scale * gain_vmem[...].astype(F32).reshape(ROWS, COLS)).astype(BF16)
    normed_out[...] = normed


def gates_of(x, router, ids, parity, expert):
    shape = (2 * CHIPS, 2 * CHIPS)
    row = lax.broadcasted_iota(jnp.int32, shape, 0)
    other = (row >= CHIPS).astype(jnp.int32)
    token = 2 * (row - other * CHIPS) + (parity + other - 2 * parity * other)
    pick = (token == lax.broadcasted_iota(jnp.int32, shape, 1)).astype(F32).astype(BF16)
    wide_ids = jnp.concatenate([ids[...].astype(F32), jnp.zeros((6, 2 * CHIPS), F32)], axis=0).astype(BF16)
    mine = dot_nt(pick, wide_ids).astype(jnp.int32)
    first, second = mine[:, 0:1], mine[:, 1:2]
    logits = dot_nt(x, router[...])
    lane = lax.broadcasted_iota(jnp.int32, logits.shape, 1)
    logit_a = jnp.sum(jnp.where(lane == first, logits, 0.0), axis=1, keepdims=True)
    logit_b = jnp.sum(jnp.where(lane == second, logits, 0.0), axis=1, keepdims=True)
    peak = jnp.maximum(logit_a, logit_b)
    exp_a, exp_b = jnp.exp(logit_a - peak), jnp.exp(logit_b - peak)
    chosen = jnp.where(first == expert, exp_a, 0.0) + jnp.where(second == expert, exp_b, 0.0)
    return chosen / (exp_a + exp_b)


def pass_kernel(normed, *refs):
    refs[-1][...] = normed[...]


def spread_kernel(normed, *refs):
    sent = refs[-1]
    sent[...] = jnp.broadcast_to(normed[...][None], sent.shape)


def expert_kernel(own, other, ids, router, gate, up, down, out_own, out_other, rows):
    core = lax.axis_index("core")
    expert = 2 * lax.axis_index("y") + core
    rows[:CHIPS] = own[...].reshape(CHIPS, D)
    rows[CHIPS:] = other[...].reshape(CHIPS, D)
    x = rows[...]
    weight = gates_of(x, router, ids, core, expert)
    g = dot(x, gate[0])
    u = dot(x, up[0])
    act = (g * jax.nn.sigmoid(g) * u).astype(BF16)
    for s in range(ROWS):
        cols = slice(s * COLS, (s + 1) * COLS)
        rows[:, cols] = (dot(act, down[0, :, cols]) * weight).astype(BF16)
    out_own[...] = rows[:CHIPS].reshape(out_own.shape)
    out_other[...] = rows[CHIPS:].reshape(out_other.shape)


def add_kernel(a, b, out):
    out[...] = (a[...].astype(F32) + b[...].astype(F32)).astype(BF16)


def finish_kernel(parts, hidden, out):
    total = jnp.sum(parts[...].astype(F32), axis=0) + hidden[...]
    for s in range(ROWS):
        out[0:1, s * COLS : (s + 1) * COLS] = total[s : s + 1, :].astype(BF16)


def swap_cores(x):
    return lax.ppermute(x, "core", [(0, 1), (1, 0)])


def params(mib):
    return pltpu.CompilerParams(vmem_limit_bytes=mib * MIB)


def in_vmem(x):
    return pltpu.with_memory_space_constraint(x, pltpu.VMEM)


def in_hbm(x):
    return pltpu.with_memory_space_constraint(x, pltpu.HBM)


def body(
    hidden_in, query, key_latent, value_latent, lengths, key_up, value_up,
    norm_gain, router_weight, route_ids, gate_weight, up_weight, down_weight,
):
    router = router_weight.T
    ids = route_ids.T
    block = (CHIPS, ROWS, COLS)
    token = jax.ShapeDtypeStruct(block, BF16)
    normed, hidden = pl.pallas_call(
        attend_kernel,
        out_shape=(
            jax.ShapeDtypeStruct((ROWS, COLS), BF16),
            jax.ShapeDtypeStruct((ROWS, COLS), F32),
        ),
        in_specs=[SMEM] + [ANY] * 7,
        out_specs=(VMEM, VMEM),
        scratch_shapes=[
            pltpu.VMEM((ROWS, COLS), F32),
            pltpu.VMEM((1, D), BF16),
            pltpu.VMEM((1, D), BF16),
            pltpu.VMEM((D,), BF16),
            pltpu.VMEM((CTX, RANK), BF16),
            pltpu.VMEM((CTX, RANK), BF16),
            pltpu.VMEM((RANK, KV_HEADS * HEAD_DIM), BF16),
            pltpu.VMEM((RANK, KV_HEADS * HEAD_DIM), BF16),
            pltpu.SemaphoreType.DMA((3,)),
            pltpu.SemaphoreType.DMA((4,)),
        ],
        compiler_params=params(16),
        name="attend",
    )(
        lengths, in_hbm(query), in_hbm(hidden_in), in_hbm(norm_gain),
        in_hbm(key_latent), in_hbm(value_latent), in_hbm(key_up), in_hbm(value_up),
    )
    held = [in_hbm(w) for w in (gate_weight, up_weight, down_weight)]
    normed = pl.pallas_call(
        pass_kernel,
        out_shape=jax.ShapeDtypeStruct((ROWS, COLS), BF16),
        in_specs=[VMEM] + [ANY] * 3,
        out_specs=VMEM,
        compiler_params=params(2),
        name="pass_on",
    )(normed, *held)
    sent = pl.pallas_call(
        spread_kernel,
        out_shape=token,
        in_specs=[VMEM] + [ANY] * 3,
        out_specs=VMEM,
        compiler_params=params(2),
        name="spread",
    )(normed, *held)
    own = lax.all_to_all(sent, CHIP_AXES, 0, 0, tiled=True)
    other = swap_cores(own)
    out_own, out_other = pl.pallas_call(
        expert_kernel,
        out_shape=(token, token),
        in_specs=[VMEM] * 7,
        out_specs=(VMEM, VMEM),
        scratch_shapes=[pltpu.VMEM((2 * CHIPS, D), BF16)],
        compiler_params=params(12),
        name="experts",
    )(own, other, ids, router, in_vmem(gate_weight), in_vmem(up_weight), in_vmem(down_weight))
    from_other = swap_cores(out_other)
    summed = pl.pallas_call(
        add_kernel,
        out_shape=token,
        in_specs=[VMEM, VMEM],
        out_specs=VMEM,
        compiler_params=params(4),
        name="add_cores",
    )(out_own, from_other)
    parts = lax.all_to_all(summed, CHIP_AXES, 0, 0, tiled=True)
    return pl.pallas_call(
        finish_kernel,
        out_shape=jax.ShapeDtypeStruct((1, D), BF16),
        in_specs=[VMEM, VMEM],
        out_specs=VMEM,
        compiler_params=params(4),
        name="finish",
    )(parts, hidden)


def solution(mesh):
    fine = Mesh(mesh.devices.reshape(4, 4, 4, 2), ALL_AXES)
    in_specs = (
        P(ALL_AXES, None),
        P(ALL_AXES, None),
        P(ALL_AXES, None, None),
        P(ALL_AXES, None, None),
        P(ALL_AXES),
        P(),
        P(),
        P(),
        P(),
        P(),
        P(("y", "core"), None, ("z", "x")),
        P(("y", "core"), None, ("z", "x")),
        P(("y", "core"), ("z", "x"), None),
    )
    return jax.shard_map(
        body, mesh=fine, in_specs=in_specs, out_specs=P(ALL_AXES, None), check_vma=False
    )
```

```python
import jax
import jax.numpy as jnp
from jax import lax
from jax.experimental import pallas as pl
from jax.experimental.pallas import tpu as pltpu
from jax.sharding import Mesh, PartitionSpec as P

KV_HEADS = 8
GROUP = 4
HEADS = KV_HEADS * GROUP
HEAD_DIM = 128
RANK = 512
CTX = 1024
D = 4096
HIDDEN = 896
ROWS = 8
COLS = 512
CHIPS = 64
CHIP_AXES = ('x', 'y', 'z')
ALL_AXES = ("z", "x", "y", "core")
F32 = jnp.float32
BF16 = jnp.bfloat16
VMEM = pl.BlockSpec(memory_space=pltpu.VMEM)
SMEM = pl.BlockSpec(memory_space=pltpu.SMEM)
ANY = pl.BlockSpec(memory_space=pl.ANY)
MIB = 2**20


def parts_of(x, n):
    out = []
    for _ in range(n):
        p = x.astype(BF16)
        out.append(p)
        x = x - p.astype(F32)
    return out


def dot_nt(a, b):
    return lax.dot_general(a, b, (((1,), (1,)), ((), ())), preferred_element_type=F32)


def dot(a, b):
    return jnp.dot(a, b, preferred_element_type=F32)


def to_rows(ref, scratch):
    for s in range(ROWS):
        scratch[s : s + 1, :] = ref[0:1, s * COLS : (s + 1) * COLS].astype(F32)
    return scratch[...]


def attend_kernel(
    length, query, hidden_in, gain, key_latent, value_latent, key_up, value_up,
    normed_out, hidden_out,
    rows_scratch, q_vmem, h_vmem, gain_vmem, kl_vmem, vl_vmem, ku_vmem, vu_vmem, small_sem, sem,
):
    small = [
        pltpu.make_async_copy(query, q_vmem, small_sem.at[0]),
        pltpu.make_async_copy(hidden_in, h_vmem, small_sem.at[1]),
        pltpu.make_async_copy(gain, gain_vmem, small_sem.at[2]),
    ]
    big = [
        pltpu.make_async_copy(src, dst, sem.at[i])
        for i, (src, dst) in enumerate(
            ((key_up, ku_vmem), (key_latent.at[0], kl_vmem), (value_latent.at[0], vl_vmem), (value_up, vu_vmem))
        )
    ]
    for c in (small[0], big[0], big[1], small[1], small[2]):
        c.start()
    small[0].wait()
    big[2].start()
    big[3].start()

    q = to_rows(q_vmem, rows_scratch)
    kv_row = lax.broadcasted_iota(jnp.int32, (KV_HEADS, KV_HEADS * HEAD_DIM), 0)
    kv_col = lax.broadcasted_iota(jnp.int32, (KV_HEADS, KV_HEADS * HEAD_DIM), 1) // HEAD_DIM
    own_block = kv_row == kv_col
    spread = []
    for g in range(GROUP):
        piece = q[:, g * HEAD_DIM : (g + 1) * HEAD_DIM]
        spread.append(jnp.where(own_block, jnp.concatenate([piece] * KV_HEADS, axis=1), 0.0))
    spread = jnp.concatenate(spread, axis=0).astype(BF16)
    big[0].wait()
    folded = dot_nt(spread, ku_vmem[...])
    stacked = jnp.concatenate(parts_of(folded, 3), axis=0)
    big[1].wait()
    s3 = dot_nt(stacked, kl_vmem[...])
    scores = (s3[:HEADS] + s3[HEADS : 2 * HEADS] + s3[2 * HEADS :]) * HEAD_DIM ** (-0.5)
    usable = lax.broadcasted_iota(jnp.int32, (HEADS, CTX), 1) < length[0]
    scores = jnp.where(usable, scores, -1e30)
    peak = jnp.max(scores, axis=1, keepdims=True)
    weights = jnp.where(usable, jnp.exp(scores - peak), 0.0)
    total = jnp.sum(weights, axis=1, keepdims=True)
    w2 = jnp.concatenate(parts_of(weights, 2), axis=0)
    big[2].wait()
    l2 = dot(w2, vl_vmem[...])
    latent = (l2[:HEADS] + l2[HEADS:]) / total
    big[3].wait()
    v2 = dot(jnp.concatenate(parts_of(latent, 2), axis=0), vu_vmem[...])
    values = v2[:HEADS] + v2[HEADS:]
    attended = []
    for g in range(GROUP):
        mine = jnp.where(own_block, values[g * KV_HEADS : (g + 1) * KV_HEADS], 0.0)
        acc = mine[:, :HEAD_DIM]
        for k in range(1, KV_HEADS):
            acc = acc + mine[:, k * HEAD_DIM : (k + 1) * HEAD_DIM]
        attended.append(acc)
    attended = jnp.concatenate(attended, axis=1)
    small[1].wait()
    small[2].wait()
    hidden = (to_rows(h_vmem, rows_scratch) + attended).astype(BF16).astype(F32)
    hidden_out[...] = hidden
    square = jnp.sum(jnp.sum(hidden * hidden, axis=1, keepdims=True), axis=0, keepdims=True)
    scale = lax.rsqrt(square * (1.0 / D) + 1e-05)
    normed = (hidden * scale * gain_vmem[...].astype(F32).reshape(ROWS, COLS)).astype(BF16)
    normed_out[...] = normed


def gates_of(x, router, ids, parity, expert):
    shape = (2 * CHIPS, 2 * CHIPS)
    row = lax.broadcasted_iota(jnp.int32, shape, 0)
    other = (row >= CHIPS).astype(jnp.int32)
    place = row - other * CHIPS
    digits = dict(zip(CHIP_AXES, (place // 16, (place // 4) % 4, place % 4)))
    chip = digits["z"] * 16 + digits["x"] * 4 + digits["y"]
    token = 2 * chip + (parity + other - 2 * parity * other)
    pick = (token == lax.broadcasted_iota(jnp.int32, shape, 1)).astype(F32).astype(BF16)
    wide_ids = jnp.concatenate([ids[...].astype(F32), jnp.zeros((6, 2 * CHIPS), F32)], axis=0).astype(BF16)
    mine = dot_nt(pick, wide_ids).astype(jnp.int32)
    first, second = mine[:, 0:1], mine[:, 1:2]
    logits = dot_nt(x, router[...])
    lane = lax.broadcasted_iota(jnp.int32, logits.shape, 1)
    logit_a = jnp.sum(jnp.where(lane == first, logits, 0.0), axis=1, keepdims=True)
    logit_b = jnp.sum(jnp.where(lane == second, logits, 0.0), axis=1, keepdims=True)
    peak = jnp.maximum(logit_a, logit_b)
    exp_a, exp_b = jnp.exp(logit_a - peak), jnp.exp(logit_b - peak)
    chosen = jnp.where(first == expert, exp_a, 0.0) + jnp.where(second == expert, exp_b, 0.0)
    return chosen / (exp_a + exp_b)


def pass_kernel(normed, *refs):
    refs[-1][...] = normed[...]


def spread_kernel(normed, *refs):
    sent = refs[-1]
    sent[...] = jnp.broadcast_to(normed[...][None], sent.shape)


def expert_kernel(own, other, ids, router, gate, up, down, out_own, out_other, rows):
    core = lax.axis_index("core")
    expert = 2 * lax.axis_index("y") + core
    rows[:CHIPS] = own[...].reshape(CHIPS, D)
    rows[CHIPS:] = other[...].reshape(CHIPS, D)
    x = rows[...]
    weight = gates_of(x, router, ids, core, expert)
    g = dot(x, gate[0])
    u = dot(x, up[0])
    act = (g * jax.nn.sigmoid(g) * u).astype(BF16)
    for s in range(ROWS):
        cols = slice(s * COLS, (s + 1) * COLS)
        rows[:, cols] = (dot(act, down[0, :, cols]) * weight).astype(BF16)
    out_own[...] = rows[:CHIPS].reshape(out_own.shape)
    out_other[...] = rows[CHIPS:].reshape(out_other.shape)


def add_kernel(a, b, out):
    out[...] = (a[...].astype(F32) + b[...].astype(F32)).astype(BF16)


def finish_kernel(parts, hidden, out):
    total = jnp.sum(parts[...].astype(F32), axis=0) + hidden[...]
    for s in range(ROWS):
        out[0:1, s * COLS : (s + 1) * COLS] = total[s : s + 1, :].astype(BF16)


def swap_cores(x):
    return lax.ppermute(x, "core", [(0, 1), (1, 0)])


def params(mib):
    return pltpu.CompilerParams(vmem_limit_bytes=mib * MIB)


def in_vmem(x):
    return pltpu.with_memory_space_constraint(x, pltpu.VMEM)


def in_hbm(x):
    return pltpu.with_memory_space_constraint(x, pltpu.HBM)


def body(
    hidden_in, query, key_latent, value_latent, lengths, key_up, value_up,
    norm_gain, router_weight, route_ids, gate_weight, up_weight, down_weight,
):
    router = router_weight.T
    ids = route_ids.T
    block = (CHIPS, ROWS, COLS)
    token = jax.ShapeDtypeStruct(block, BF16)
    normed, hidden = pl.pallas_call(
        attend_kernel,
        out_shape=(
            jax.ShapeDtypeStruct((ROWS, COLS), BF16),
            jax.ShapeDtypeStruct((ROWS, COLS), F32),
        ),
        in_specs=[SMEM] + [ANY] * 7,
        out_specs=(VMEM, VMEM),
        scratch_shapes=[
            pltpu.VMEM((ROWS, COLS), F32),
            pltpu.VMEM((1, D), BF16),
            pltpu.VMEM((1, D), BF16),
            pltpu.VMEM((D,), BF16),
            pltpu.VMEM((CTX, RANK), BF16),
            pltpu.VMEM((CTX, RANK), BF16),
            pltpu.VMEM((RANK, KV_HEADS * HEAD_DIM), BF16),
            pltpu.VMEM((RANK, KV_HEADS * HEAD_DIM), BF16),
            pltpu.SemaphoreType.DMA((3,)),
            pltpu.SemaphoreType.DMA((4,)),
        ],
        compiler_params=params(16),
        name="attend",
    )(
        lengths, in_hbm(query), in_hbm(hidden_in), in_hbm(norm_gain),
        in_hbm(key_latent), in_hbm(value_latent), in_hbm(key_up), in_hbm(value_up),
    )
    held = [in_hbm(w) for w in (gate_weight, up_weight, down_weight)]
    normed = pl.pallas_call(
        pass_kernel,
        out_shape=jax.ShapeDtypeStruct((ROWS, COLS), BF16),
        in_specs=[VMEM] + [ANY] * 3,
        out_specs=VMEM,
        compiler_params=params(2),
        name="pass_on",
    )(normed, *held)
    sent = pl.pallas_call(
        spread_kernel,
        out_shape=token,
        in_specs=[VMEM] + [ANY] * 3,
        out_specs=VMEM,
        compiler_params=params(2),
        name="spread",
    )(normed, *held)
    own = lax.all_to_all(sent, CHIP_AXES, 0, 0, tiled=True)
    other = swap_cores(own)
    out_own, out_other = pl.pallas_call(
        expert_kernel,
        out_shape=(token, token),
        in_specs=[VMEM] * 7,
        out_specs=(VMEM, VMEM),
        scratch_shapes=[pltpu.VMEM((2 * CHIPS, D), BF16)],
        compiler_params=params(12),
        name="experts",
    )(own, other, ids, router, in_vmem(gate_weight), in_vmem(up_weight), in_vmem(down_weight))
    from_other = swap_cores(out_other)
    summed = pl.pallas_call(
        add_kernel,
        out_shape=token,
        in_specs=[VMEM, VMEM],
        out_specs=VMEM,
        compiler_params=params(4),
        name="add_cores",
    )(out_own, from_other)
    parts = lax.all_to_all(summed, CHIP_AXES, 0, 0, tiled=True)
    return pl.pallas_call(
        finish_kernel,
        out_shape=jax.ShapeDtypeStruct((1, D), BF16),
        in_specs=[VMEM, VMEM],
        out_specs=VMEM,
        compiler_params=params(4),
        name="finish",
    )(parts, hidden)


def solution(mesh):
    fine = Mesh(mesh.devices.reshape(4, 4, 4, 2), ALL_AXES)
    in_specs = (
        P(ALL_AXES, None),
        P(ALL_AXES, None),
        P(ALL_AXES, None, None),
        P(ALL_AXES, None, None),
        P(ALL_AXES),
        P(),
        P(),
        P(),
        P(),
        P(),
        P(("y", "core"), None, ("z", "x")),
        P(("y", "core"), None, ("z", "x")),
        P(("y", "core"), ("z", "x"), None),
    )
    return jax.shard_map(
        body, mesh=fine, in_specs=in_specs, out_specs=P(ALL_AXES, None), check_vma=False
    )
```

```python
import jax
import jax.numpy as jnp
from jax import lax
from jax.experimental import pallas as pl
from jax.experimental.pallas import tpu as pltpu
from jax.sharding import Mesh, PartitionSpec as P

KV_HEADS = 8
GROUP = 4
HEADS = KV_HEADS * GROUP
HEAD_DIM = 128
RANK = 512
CTX = 1024
D = 4096
HIDDEN = 896
ROWS = 8
COLS = 512
CHIPS = 64
CHIP_AXES = ('x', 'y', 'z')
ALL_AXES = ("z", "x", "y", "core")
F32 = jnp.float32
BF16 = jnp.bfloat16
VMEM = pl.BlockSpec(memory_space=pltpu.VMEM)
SMEM = pl.BlockSpec(memory_space=pltpu.SMEM)
ANY = pl.BlockSpec(memory_space=pl.ANY)
MIB = 2**20


def parts_of(x, n):
    out = []
    for _ in range(n):
        p = x.astype(BF16)
        out.append(p)
        x = x - p.astype(F32)
    return out


def dot_nt(a, b):
    return lax.dot_general(a, b, (((1,), (1,)), ((), ())), preferred_element_type=F32)


def dot(a, b):
    return jnp.dot(a, b, preferred_element_type=F32)


def to_rows(ref, scratch):
    for s in range(ROWS):
        scratch[s : s + 1, :] = ref[0:1, s * COLS : (s + 1) * COLS].astype(F32)
    return scratch[...]


def attend_kernel(
    length, query, hidden_in, gain, key_latent, value_latent, key_up, value_up,
    normed_out, hidden_out,
    rows_scratch, q_vmem, h_vmem, gain_vmem, kl_vmem, vl_vmem, ku_vmem, vu_vmem, small_sem, sem,
):
    small = [
        pltpu.make_async_copy(query, q_vmem, small_sem.at[0]),
        pltpu.make_async_copy(hidden_in, h_vmem, small_sem.at[1]),
        pltpu.make_async_copy(gain, gain_vmem, small_sem.at[2]),
    ]
    big = [
        pltpu.make_async_copy(src, dst, sem.at[i])
        for i, (src, dst) in enumerate(
            ((key_up, ku_vmem), (key_latent.at[0], kl_vmem), (value_latent.at[0], vl_vmem), (value_up, vu_vmem))
        )
    ]
    for c in (small[0], big[0], big[1], small[1], small[2]):
        c.start()
    small[0].wait()
    big[2].start()
    big[3].start()

    q = to_rows(q_vmem, rows_scratch)
    kv_row = lax.broadcasted_iota(jnp.int32, (KV_HEADS, KV_HEADS * HEAD_DIM), 0)
    kv_col = lax.broadcasted_iota(jnp.int32, (KV_HEADS, KV_HEADS * HEAD_DIM), 1) // HEAD_DIM
    own_block = kv_row == kv_col
    spread = []
    for g in range(GROUP):
        piece = q[:, g * HEAD_DIM : (g + 1) * HEAD_DIM]
        spread.append(jnp.where(own_block, jnp.concatenate([piece] * KV_HEADS, axis=1), 0.0))
    spread = jnp.concatenate(spread, axis=0).astype(BF16)
    big[0].wait()
    folded = dot_nt(spread, ku_vmem[...])
    stacked = jnp.concatenate(parts_of(folded, 3), axis=0)
    big[1].wait()
    s3 = dot_nt(stacked, kl_vmem[...])
    scores = (s3[:HEADS] + s3[HEADS : 2 * HEADS] + s3[2 * HEADS :]) * HEAD_DIM ** (-0.5)
    usable = lax.broadcasted_iota(jnp.int32, (HEADS, CTX), 1) < length[0]
    scores = jnp.where(usable, scores, -1e30)
    peak = jnp.max(scores, axis=1, keepdims=True)
    weights = jnp.where(usable, jnp.exp(scores - peak), 0.0)
    total = jnp.sum(weights, axis=1, keepdims=True)
    w2 = jnp.concatenate(parts_of(weights, 2), axis=0)
    big[2].wait()
    l2 = dot(w2, vl_vmem[...])
    latent = (l2[:HEADS] + l2[HEADS:]) / total
    big[3].wait()
    v2 = dot(jnp.concatenate(parts_of(latent, 2), axis=0), vu_vmem[...])
    values = v2[:HEADS] + v2[HEADS:]
    attended = []
    for g in range(GROUP):
        mine = jnp.where(own_block, values[g * KV_HEADS : (g + 1) * KV_HEADS], 0.0)
        acc = mine[:, :HEAD_DIM]
        for k in range(1, KV_HEADS):
            acc = acc + mine[:, k * HEAD_DIM : (k + 1) * HEAD_DIM]
        attended.append(acc)
    attended = jnp.concatenate(attended, axis=1)
    small[1].wait()
    small[2].wait()
    hidden = (to_rows(h_vmem, rows_scratch) + attended).astype(BF16).astype(F32)
    hidden_out[...] = hidden
    square = jnp.sum(jnp.sum(hidden * hidden, axis=1, keepdims=True), axis=0, keepdims=True)
    scale = lax.rsqrt(square * (1.0 / D) + 1e-05)
    normed = (hidden * scale * gain_vmem[...].astype(F32).reshape(ROWS, COLS)).astype(BF16)
    normed_out[...] = normed


def gates_of(x, router, ids, parity, expert):
    shape = (CHIPS, 2 * CHIPS)
    place = lax.broadcasted_iota(jnp.int32, shape, 0)
    digits = dict(zip(CHIP_AXES, (place // 16, (place // 4) % 4, place % 4)))
    token = 2 * (digits["z"] * 16 + digits["x"] * 4 + digits["y"]) + parity
    pick = (token == lax.broadcasted_iota(jnp.int32, shape, 1)).astype(F32).astype(BF16)
    wide_ids = jnp.concatenate([ids[...].astype(F32), jnp.zeros((6, 2 * CHIPS), F32)], axis=0).astype(BF16)
    mine = dot_nt(pick, wide_ids).astype(jnp.int32)
    first, second = mine[:, 0:1], mine[:, 1:2]
    logits = dot_nt(x, router[...])
    lane = lax.broadcasted_iota(jnp.int32, logits.shape, 1)
    logit_a = jnp.sum(jnp.where(lane == first, logits, 0.0), axis=1, keepdims=True)
    logit_b = jnp.sum(jnp.where(lane == second, logits, 0.0), axis=1, keepdims=True)
    peak = jnp.maximum(logit_a, logit_b)
    exp_a, exp_b = jnp.exp(logit_a - peak), jnp.exp(logit_b - peak)
    chosen = jnp.where(first == expert, exp_a, 0.0) + jnp.where(second == expert, exp_b, 0.0)
    return chosen / (exp_a + exp_b)


def pass_kernel(normed, *refs):
    refs[-1][...] = normed[...]


def spread_kernel(normed, *refs):
    sent = refs[-1]
    sent[...] = jnp.broadcast_to(normed[...][None], sent.shape)


def own_kernel(own, ids, router, rows_out, weight_out):
    core = lax.axis_index("core")
    x = own[...].reshape(CHIPS, D)
    rows_out[...] = x
    weight = gates_of(x, router, ids, core, 2 * lax.axis_index("y") + core)
    weight_out[...] = jnp.broadcast_to(weight, weight_out.shape)


def expert_kernel(
    own_rows, own_weight, other, ids, router, gate, up, down,
    out_own, out_other, rows,
):
    core = lax.axis_index("core")
    rows[:CHIPS] = own_rows[...]
    rows[CHIPS:] = other[...].reshape(CHIPS, D)
    x = rows[...]
    other_weight = gates_of(rows[CHIPS:], router, ids, 1 - core, 2 * lax.axis_index("y") + core)
    weight = jnp.concatenate([own_weight[:, :1], other_weight], axis=0)
    g = dot(x, gate[0])
    u = dot(x, up[0])
    act = (g * jax.nn.sigmoid(g) * u).astype(BF16)
    for s in range(ROWS):
        cols = slice(s * COLS, (s + 1) * COLS)
        part = (dot(act, down[0, :, cols]) * weight).astype(BF16)
        out_own[:, cols] = part[:CHIPS]
        rows[CHIPS:, cols] = part[CHIPS:]
    out_other[...] = rows[CHIPS:].reshape(out_other.shape)


def blocks_kernel(rows, out):
    out[...] = rows[...].reshape(out.shape)


def add_kernel(a, b, out):
    out[...] = (a[...].astype(F32) + b[...].astype(F32)).astype(BF16)


def finish_kernel(parts, hidden, out):
    total = jnp.sum(parts[...].astype(F32), axis=0) + hidden[...]
    for s in range(ROWS):
        out[0:1, s * COLS : (s + 1) * COLS] = total[s : s + 1, :].astype(BF16)


def swap_cores(x):
    return lax.ppermute(x, "core", [(0, 1), (1, 0)])


def params(mib):
    return pltpu.CompilerParams(vmem_limit_bytes=mib * MIB)


def in_vmem(x):
    return pltpu.with_memory_space_constraint(x, pltpu.VMEM)


def in_hbm(x):
    return pltpu.with_memory_space_constraint(x, pltpu.HBM)


def body(
    hidden_in, query, key_latent, value_latent, lengths, key_up, value_up,
    norm_gain, router_weight, route_ids, gate_weight, up_weight, down_weight,
):
    router = router_weight.T
    ids = route_ids.T
    block = (CHIPS, ROWS, COLS)
    token = jax.ShapeDtypeStruct(block, BF16)
    normed, hidden = pl.pallas_call(
        attend_kernel,
        out_shape=(
            jax.ShapeDtypeStruct((ROWS, COLS), BF16),
            jax.ShapeDtypeStruct((ROWS, COLS), F32),
        ),
        in_specs=[SMEM] + [ANY] * 7,
        out_specs=(VMEM, VMEM),
        scratch_shapes=[
            pltpu.VMEM((ROWS, COLS), F32),
            pltpu.VMEM((1, D), BF16),
            pltpu.VMEM((1, D), BF16),
            pltpu.VMEM((D,), BF16),
            pltpu.VMEM((CTX, RANK), BF16),
            pltpu.VMEM((CTX, RANK), BF16),
            pltpu.VMEM((RANK, KV_HEADS * HEAD_DIM), BF16),
            pltpu.VMEM((RANK, KV_HEADS * HEAD_DIM), BF16),
            pltpu.SemaphoreType.DMA((3,)),
            pltpu.SemaphoreType.DMA((4,)),
        ],
        compiler_params=params(16),
        name="attend",
    )(
        lengths, in_hbm(query), in_hbm(hidden_in), in_hbm(norm_gain),
        in_hbm(key_latent), in_hbm(value_latent), in_hbm(key_up), in_hbm(value_up),
    )
    held = [in_hbm(w) for w in (gate_weight, up_weight, down_weight)]
    normed = pl.pallas_call(
        pass_kernel,
        out_shape=jax.ShapeDtypeStruct((ROWS, COLS), BF16),
        in_specs=[VMEM] + [ANY] * 3,
        out_specs=VMEM,
        compiler_params=params(2),
        name="pass_on",
    )(normed, *held)
    sent = pl.pallas_call(
        spread_kernel,
        out_shape=token,
        in_specs=[VMEM] + [ANY] * 3,
        out_specs=VMEM,
        compiler_params=params(2),
        name="spread",
    )(normed, *held)
    own = lax.all_to_all(sent, CHIP_AXES, 0, 0, tiled=True)
    other = swap_cores(own)
    own_rows, own_weight = pl.pallas_call(
        own_kernel,
        out_shape=(
            jax.ShapeDtypeStruct((CHIPS, D), BF16),
            jax.ShapeDtypeStruct((CHIPS, HEAD_DIM), F32),
        ),
        in_specs=[VMEM] * 3,
        out_specs=(VMEM,) * 2,
        compiler_params=params(4),
        cost_estimate=pl.CostEstimate(flops=0, bytes_accessed=2 * MIB, transcendentals=0),
        name="own_rows",
    )(own, ids, router)
    out_own, out_other = pl.pallas_call(
        expert_kernel,
        out_shape=(jax.ShapeDtypeStruct((CHIPS, D), BF16), token),
        in_specs=[VMEM] * 8,
        out_specs=(VMEM, VMEM),
        scratch_shapes=[pltpu.VMEM((2 * CHIPS, D), BF16)],
        compiler_params=params(12),
        name="experts",
    )(
        own_rows, own_weight, other, ids, router,
        in_vmem(gate_weight), in_vmem(up_weight), in_vmem(down_weight),
    )
    from_other = swap_cores(out_other)
    out_own = pl.pallas_call(
        blocks_kernel,
        out_shape=token,
        in_specs=[VMEM],
        out_specs=VMEM,
        compiler_params=params(4),
        cost_estimate=pl.CostEstimate(flops=0, bytes_accessed=2 * MIB, transcendentals=0),
        name="own_blocks",
    )(out_own)
    summed = pl.pallas_call(
        add_kernel,
        out_shape=token,
        in_specs=[VMEM, VMEM],
        out_specs=VMEM,
        compiler_params=params(4),
        name="add_cores",
    )(out_own, from_other)
    parts = lax.all_to_all(summed, CHIP_AXES, 0, 0, tiled=True)
    return pl.pallas_call(
        finish_kernel,
        out_shape=jax.ShapeDtypeStruct((1, D), BF16),
        in_specs=[VMEM, VMEM],
        out_specs=VMEM,
        compiler_params=params(4),
        name="finish",
    )(parts, hidden)


def solution(mesh):
    fine = Mesh(mesh.devices.reshape(4, 4, 4, 2), ALL_AXES)
    in_specs = (
        P(ALL_AXES, None),
        P(ALL_AXES, None),
        P(ALL_AXES, None, None),
        P(ALL_AXES, None, None),
        P(ALL_AXES),
        P(),
        P(),
        P(),
        P(),
        P(),
        P(("y", "core"), None, ("z", "x")),
        P(("y", "core"), None, ("z", "x")),
        P(("y", "core"), ("z", "x"), None),
    )
    return jax.shard_map(
        body, mesh=fine, in_specs=in_specs, out_specs=P(ALL_AXES, None), check_vma=False
    )
```

```python
import jax
import jax.numpy as jnp
from jax import lax
from jax.experimental import pallas as pl
from jax.experimental.pallas import tpu as pltpu
from jax.sharding import Mesh, PartitionSpec as P

KV_HEADS = 8
GROUP = 4
HEADS = KV_HEADS * GROUP
HEAD_DIM = 128
RANK = 512
CTX = 1024
D = 4096
HIDDEN = 896
ROWS = 8
COLS = 512
CHIPS = 64
CHIP_AXES = ('x', 'y', 'z')
ALL_AXES = ("z", "x", "y", "core")
F32 = jnp.float32
BF16 = jnp.bfloat16
VMEM = pl.BlockSpec(memory_space=pltpu.VMEM)
SMEM = pl.BlockSpec(memory_space=pltpu.SMEM)
ANY = pl.BlockSpec(memory_space=pl.ANY)
MIB = 2**20


def parts_of(x, n):
    out = []
    for _ in range(n):
        p = x.astype(BF16)
        out.append(p)
        x = x - p.astype(F32)
    return out


def dot_nt(a, b):
    return lax.dot_general(a, b, (((1,), (1,)), ((), ())), preferred_element_type=F32)


def dot(a, b):
    return jnp.dot(a, b, preferred_element_type=F32)


def to_rows(ref, scratch):
    for s in range(ROWS):
        scratch[s : s + 1, :] = ref[0:1, s * COLS : (s + 1) * COLS].astype(F32)
    return scratch[...]


def attend_kernel(
    length, query, hidden_in, gain, key_latent, value_latent, key_up, value_up,
    normed_out, hidden_out,
    rows_scratch, q_vmem, h_vmem, gain_vmem, kl_vmem, vl_vmem, ku_vmem, vu_vmem, small_sem, sem,
):
    small = [
        pltpu.make_async_copy(query, q_vmem, small_sem.at[0]),
        pltpu.make_async_copy(hidden_in, h_vmem, small_sem.at[1]),
        pltpu.make_async_copy(gain, gain_vmem, small_sem.at[2]),
    ]
    big = [
        pltpu.make_async_copy(src, dst, sem.at[i])
        for i, (src, dst) in enumerate(
            ((key_up, ku_vmem), (key_latent.at[0], kl_vmem), (value_latent.at[0], vl_vmem), (value_up, vu_vmem))
        )
    ]
    for c in (small[0], big[0], big[1], small[1], small[2]):
        c.start()
    small[0].wait()
    big[2].start()
    big[3].start()

    q = to_rows(q_vmem, rows_scratch)
    kv_row = lax.broadcasted_iota(jnp.int32, (KV_HEADS, KV_HEADS * HEAD_DIM), 0)
    kv_col = lax.broadcasted_iota(jnp.int32, (KV_HEADS, KV_HEADS * HEAD_DIM), 1) // HEAD_DIM
    own_block = kv_row == kv_col
    spread = []
    for g in range(GROUP):
        piece = q[:, g * HEAD_DIM : (g + 1) * HEAD_DIM]
        spread.append(jnp.where(own_block, jnp.concatenate([piece] * KV_HEADS, axis=1), 0.0))
    spread = jnp.concatenate(spread, axis=0).astype(BF16)
    big[0].wait()
    folded = dot_nt(spread, ku_vmem[...])
    stacked = jnp.concatenate(parts_of(folded, 3), axis=0)
    big[1].wait()
    s3 = dot_nt(stacked, kl_vmem[...])
    scores = (s3[:HEADS] + s3[HEADS : 2 * HEADS] + s3[2 * HEADS :]) * HEAD_DIM ** (-0.5)
    usable = lax.broadcasted_iota(jnp.int32, (HEADS, CTX), 1) < length[0]
    scores = jnp.where(usable, scores, -1e30)
    peak = jnp.max(scores, axis=1, keepdims=True)
    weights = jnp.where(usable, jnp.exp(scores - peak), 0.0)
    total = jnp.sum(weights, axis=1, keepdims=True)
    w2 = jnp.concatenate(parts_of(weights, 2), axis=0)
    big[2].wait()
    l2 = dot(w2, vl_vmem[...])
    latent = (l2[:HEADS] + l2[HEADS:]) / total
    big[3].wait()
    v2 = dot(jnp.concatenate(parts_of(latent, 2), axis=0), vu_vmem[...])
    values = v2[:HEADS] + v2[HEADS:]
    attended = []
    for g in range(GROUP):
        mine = jnp.where(own_block, values[g * KV_HEADS : (g + 1) * KV_HEADS], 0.0)
        acc = mine[:, :HEAD_DIM]
        for k in range(1, KV_HEADS):
            acc = acc + mine[:, k * HEAD_DIM : (k + 1) * HEAD_DIM]
        attended.append(acc)
    attended = jnp.concatenate(attended, axis=1)
    small[1].wait()
    small[2].wait()
    hidden = (to_rows(h_vmem, rows_scratch) + attended).astype(BF16).astype(F32)
    hidden_out[...] = hidden
    square = jnp.sum(jnp.sum(hidden * hidden, axis=1, keepdims=True), axis=0, keepdims=True)
    scale = lax.rsqrt(square * (1.0 / D) + 1e-05)
    normed = (hidden * scale * gain_vmem[...].astype(F32).reshape(ROWS, COLS)).astype(BF16)
    normed_out[...] = normed


def gates_of(x, router, ids, parity, expert):
    shape = (CHIPS, 2 * CHIPS)
    place = lax.broadcasted_iota(jnp.int32, shape, 0)
    digits = dict(zip(CHIP_AXES, (place // 16, (place // 4) % 4, place % 4)))
    token = 2 * (digits["z"] * 16 + digits["x"] * 4 + digits["y"]) + parity
    pick = (token == lax.broadcasted_iota(jnp.int32, shape, 1)).astype(F32).astype(BF16)
    wide_ids = jnp.concatenate([ids[...].astype(F32), jnp.zeros((6, 2 * CHIPS), F32)], axis=0).astype(BF16)
    mine = dot_nt(pick, wide_ids).astype(jnp.int32)
    first, second = mine[:, 0:1], mine[:, 1:2]
    logits = dot_nt(x, router[...])
    lane = lax.broadcasted_iota(jnp.int32, logits.shape, 1)
    logit_a = jnp.sum(jnp.where(lane == first, logits, 0.0), axis=1, keepdims=True)
    logit_b = jnp.sum(jnp.where(lane == second, logits, 0.0), axis=1, keepdims=True)
    peak = jnp.maximum(logit_a, logit_b)
    exp_a, exp_b = jnp.exp(logit_a - peak), jnp.exp(logit_b - peak)
    chosen = jnp.where(first == expert, exp_a, 0.0) + jnp.where(second == expert, exp_b, 0.0)
    return chosen / (exp_a + exp_b)


def pass_kernel(normed, *refs):
    refs[-1][...] = normed[...]


def spread_kernel(normed, *refs):
    sent = refs[-1]
    sent[...] = jnp.broadcast_to(normed[...][None], sent.shape)


def own_kernel(own, ids, router, rows_out, weight_out):
    core = lax.axis_index("core")
    x = own[...].reshape(CHIPS, D)
    rows_out[...] = x
    weight = gates_of(x, router, ids, core, 2 * lax.axis_index("y") + core)
    weight_out[...] = jnp.broadcast_to(weight, weight_out.shape)


def expert_kernel(
    own_rows, own_weight, other, ids, router, gate, up, down,
    out_own, out_other, rows,
):
    core = lax.axis_index("core")
    rows[:CHIPS] = own_rows[...]
    rows[CHIPS:] = other[...].reshape(CHIPS, D)
    x = rows[...]
    other_weight = gates_of(rows[CHIPS:], router, ids, 1 - core, 2 * lax.axis_index("y") + core)
    weight = jnp.concatenate([own_weight[:, :1], other_weight], axis=0)
    g = dot(x, gate[0])
    u = dot(x, up[0])
    act = (g * jax.nn.sigmoid(g) * u).astype(BF16)
    for s in range(ROWS):
        cols = slice(s * COLS, (s + 1) * COLS)
        part = (dot(act, down[0, :, cols]) * weight).astype(BF16)
        out_own[:, cols] = part[:CHIPS]
        rows[CHIPS:, cols] = part[CHIPS:]
    out_other[...] = rows[CHIPS:].reshape(out_other.shape)


def blocks_kernel(rows, out):
    out[...] = rows[...].reshape(out.shape)


def add_kernel(a, b, out):
    out[...] = (a[...].astype(F32) + b[...].astype(F32)).astype(BF16)


def finish_kernel(parts, hidden, out):
    sums = [hidden[...]] + [jnp.zeros((ROWS, COLS), F32)] * 3
    for i in range(CHIPS):
        sums[i % 4] = sums[i % 4] + parts[i].astype(F32)
    total = (sums[0] + sums[1]) + (sums[2] + sums[3])
    for s in range(ROWS):
        out[0:1, s * COLS : (s + 1) * COLS] = total[s : s + 1, :].astype(BF16)


def swap_cores(x):
    return lax.ppermute(x, "core", [(0, 1), (1, 0)])


def params(mib):
    return pltpu.CompilerParams(vmem_limit_bytes=mib * MIB)


def in_vmem(x):
    return pltpu.with_memory_space_constraint(x, pltpu.VMEM)


def in_hbm(x):
    return pltpu.with_memory_space_constraint(x, pltpu.HBM)


def body(
    hidden_in, query, key_latent, value_latent, lengths, key_up, value_up,
    norm_gain, router_weight, route_ids, gate_weight, up_weight, down_weight,
):
    router = router_weight.T
    ids = route_ids.T
    block = (CHIPS, ROWS, COLS)
    token = jax.ShapeDtypeStruct(block, BF16)
    normed, hidden = pl.pallas_call(
        attend_kernel,
        out_shape=(
            jax.ShapeDtypeStruct((ROWS, COLS), BF16),
            jax.ShapeDtypeStruct((ROWS, COLS), F32),
        ),
        in_specs=[SMEM] + [ANY] * 7,
        out_specs=(VMEM, VMEM),
        scratch_shapes=[
            pltpu.VMEM((ROWS, COLS), F32),
            pltpu.VMEM((1, D), BF16),
            pltpu.VMEM((1, D), BF16),
            pltpu.VMEM((D,), BF16),
            pltpu.VMEM((CTX, RANK), BF16),
            pltpu.VMEM((CTX, RANK), BF16),
            pltpu.VMEM((RANK, KV_HEADS * HEAD_DIM), BF16),
            pltpu.VMEM((RANK, KV_HEADS * HEAD_DIM), BF16),
            pltpu.SemaphoreType.DMA((3,)),
            pltpu.SemaphoreType.DMA((4,)),
        ],
        compiler_params=params(16),
        name="attend",
    )(
        lengths, in_hbm(query), in_hbm(hidden_in), in_hbm(norm_gain),
        in_hbm(key_latent), in_hbm(value_latent), in_hbm(key_up), in_hbm(value_up),
    )
    held = [in_hbm(w) for w in (gate_weight, up_weight, down_weight)]
    normed = pl.pallas_call(
        pass_kernel,
        out_shape=jax.ShapeDtypeStruct((ROWS, COLS), BF16),
        in_specs=[VMEM] + [ANY] * 3,
        out_specs=VMEM,
        compiler_params=params(2),
        name="pass_on",
    )(normed, *held)
    sent = pl.pallas_call(
        spread_kernel,
        out_shape=token,
        in_specs=[VMEM] + [ANY] * 3,
        out_specs=VMEM,
        compiler_params=params(2),
        name="spread",
    )(normed, *held)
    own = lax.all_to_all(sent, CHIP_AXES, 0, 0, tiled=True)
    other = swap_cores(own)
    own_rows, own_weight = pl.pallas_call(
        own_kernel,
        out_shape=(
            jax.ShapeDtypeStruct((CHIPS, D), BF16),
            jax.ShapeDtypeStruct((CHIPS, HEAD_DIM), F32),
        ),
        in_specs=[VMEM] * 3,
        out_specs=(VMEM,) * 2,
        compiler_params=params(4),
        cost_estimate=pl.CostEstimate(flops=0, bytes_accessed=2 * MIB, transcendentals=0),
        name="own_rows",
    )(own, ids, router)
    out_own, out_other = pl.pallas_call(
        expert_kernel,
        out_shape=(jax.ShapeDtypeStruct((CHIPS, D), BF16), token),
        in_specs=[VMEM] * 8,
        out_specs=(VMEM, VMEM),
        scratch_shapes=[pltpu.VMEM((2 * CHIPS, D), BF16)],
        compiler_params=params(12),
        name="experts",
    )(
        own_rows, own_weight, other, ids, router,
        in_vmem(gate_weight), in_vmem(up_weight), in_vmem(down_weight),
    )
    from_other = swap_cores(out_other)
    out_own = pl.pallas_call(
        blocks_kernel,
        out_shape=token,
        in_specs=[VMEM],
        out_specs=VMEM,
        compiler_params=params(4),
        cost_estimate=pl.CostEstimate(flops=0, bytes_accessed=2 * MIB, transcendentals=0),
        name="own_blocks",
    )(out_own)
    summed = pl.pallas_call(
        add_kernel,
        out_shape=token,
        in_specs=[VMEM, VMEM],
        out_specs=VMEM,
        compiler_params=params(4),
        name="add_cores",
    )(out_own, from_other)
    parts = lax.all_to_all(summed, CHIP_AXES, 0, 0, tiled=True)
    return pl.pallas_call(
        finish_kernel,
        out_shape=jax.ShapeDtypeStruct((1, D), BF16),
        in_specs=[VMEM, VMEM],
        out_specs=VMEM,
        compiler_params=params(4),
        name="finish",
    )(parts, hidden)


def solution(mesh):
    fine = Mesh(mesh.devices.reshape(4, 4, 4, 2), ALL_AXES)
    in_specs = (
        P(ALL_AXES, None),
        P(ALL_AXES, None),
        P(ALL_AXES, None, None),
        P(ALL_AXES, None, None),
        P(ALL_AXES),
        P(),
        P(),
        P(),
        P(),
        P(),
        P(("y", "core"), None, ("z", "x")),
        P(("y", "core"), None, ("z", "x")),
        P(("y", "core"), ("z", "x"), None),
    )
    return jax.shard_map(
        body, mesh=fine, in_specs=in_specs, out_specs=P(ALL_AXES, None), check_vma=False
    )
```
